32 devices in a mesh: blk: 8 (over y, x, core), rep: 4 (over z).
Axes of the slice: x: 2, y: 2, z: 4, core: 2. Of those that a mesh axis runs over, the one named last changes fastest.
Arguments:
- embeddings: bfloat16 [8192, 512], P('blk'), may hold values from -1.5 to 1.5
- relation: float32 [4, 512], replicated, may hold values from 0.1 to 1.9
- head_ids: int32 [4, 8192], P(None, ('blk', 'rep')), may hold values from 0 to 1023
- context_ids: int32 [4, 8192], P(None, ('blk', 'rep')), may hold values from 0 to 1023
- neg_owner: int32 [4], replicated, may hold values from 0 to 7
- neg_ids: int32 [4, 768], replicated, may hold values from 0 to 1023
Outputs:
- embedding_grad: float32 [8192, 512], P('blk', 'rep')
The draws below stay inside these ranges and needn't reach their ends.
All inputs are finite; a program needn't handle non-finite values.
Results may differ from the reference program's by a relative error of at most 0.0055.
Values may be sent and summed in bfloat16 or wider, within the bound.
A program may use at most 128 MiB of HBM per device.

```python
import jax
import jax.numpy as jnp
from jax import lax

D = 512
PART_ROWS = 1024
EDGES = 256
NEG = 768
STOPS = 4
ENT = 8192
EDGES_ALL = 8192
N_BLK = 8
N_REP = 4


def with_ends(values, key, least, high):
    spot = [jax.random.randint(jax.random.fold_in(key, axis), (), 0, length) for axis, length in enumerate(values.shape)]
    main_axis = values.shape.index(max(values.shape))
    next_to = spot[:main_axis] + [(spot[main_axis] + 1) % values.shape[main_axis]] + spot[main_axis + 1:]
    return values.at[tuple(spot)].set(least).at[tuple(next_to)].set(high)


def steps_of(own_key, shape, pieces, smallest, largest):
    factor_of, own = 1.0, jax.random.fold_in(own_key, 6)
    for dim, shards_of in pieces:
        draws = jnp.exp(jax.random.uniform(jax.random.fold_in(own, dim), (shards_of,), jnp.float32, smallest / len(pieces), largest / len(pieces)))
        factor_of = factor_of * jnp.repeat(draws, shape[dim] // shards_of).reshape([-1 if axis == dim else 1 for axis in range(len(shape))])
    return factor_of


def scatter_about(own_key, extent, scale, reach, cuts=(), held_as=jnp.bfloat16):
    entries = jax.random.normal(own_key, extent, jnp.float32) * scale
    if len(cuts) > 0:
        entries = steps_of(own_key, extent, cuts, -0.22, 0.18) * entries
    return jnp.clip(entries, min=-reach, max=reach).astype(held_as)


def setup_inputs(seed: int = 0) -> dict:
    splits = jax.random.split(jax.random.key(seed), 7)
    embeddings = scatter_about(splits[0], (ENT, D), 0.25, 1.5, ((0, 8),))
    relation = jnp.clip(1.0 + 0.18 * jax.random.normal(splits[1], (STOPS, D), jnp.float32), 0.1, 1.9)
    head_ids = with_ends(jax.random.randint(splits[2], (STOPS, EDGES_ALL), 0, PART_ROWS), jax.random.fold_in(splits[2], 1), 0, PART_ROWS - 1).astype(jnp.int32)
    context_ids = with_ends(jax.random.randint(splits[3], (STOPS, EDGES_ALL), 0, PART_ROWS), jax.random.fold_in(splits[3], 1), 0, PART_ROWS - 1).astype(jnp.int32)
    neg_owner = with_ends(jax.random.randint(splits[4], (STOPS,), 0, N_BLK), jax.random.fold_in(splits[4], 1), 0, N_BLK - 1).astype(jnp.int32)
    neg_ids = with_ends(jax.random.randint(splits[5], (STOPS, NEG), 0, PART_ROWS), jax.random.fold_in(splits[5], 1), 0, PART_ROWS - 1).astype(jnp.int32)
    return {"embeddings": embeddings, "relation": relation, "head_ids": head_ids, "context_ids": context_ids, "neg_owner": neg_owner, "neg_ids": neg_ids}


def stop_terms(home_rows, visitor, negatives, relation_row, head_index, context_index, weight):
    head_rows = jnp.take(home_rows, head_index, axis=0)
    context_rows = jnp.take(visitor, context_index, axis=0)
    weighted = (head_rows.astype(jnp.float32) * relation_row).astype(jnp.bfloat16)
    positive = jnp.sum(weighted.astype(jnp.float32) * context_rows.astype(jnp.float32), axis=1)
    scores = lax.dot_general(weighted, negatives, (((1,), (1,)), ((), ())), preferred_element_type=jnp.float32)
    pos_grad = -jax.nn.sigmoid(-positive)
    neg_grad = (weight * jax.nn.sigmoid(scores)).astype(jnp.bfloat16)
    pulled = jnp.dot(neg_grad, negatives, preferred_element_type=jnp.float32)
    head_terms = relation_row * (pos_grad[:, None] * context_rows.astype(jnp.float32) + pulled)
    context_terms = pos_grad[:, None] * weighted.astype(jnp.float32)
    empty = jnp.zeros((home_rows.shape[0], home_rows.shape[1]), jnp.float32)
    return empty.at[head_index].add(head_terms), empty.at[context_index].add(context_terms)


def reference(embeddings, relation, head_ids, context_ids, neg_owner, neg_ids):
    weight = 4.0 / NEG
    gradient = jnp.zeros((ENT, D), jnp.float32)
    head_blocks = head_ids.reshape(STOPS, N_BLK, N_REP * EDGES)
    context_blocks = context_ids.reshape(STOPS, N_BLK, N_REP * EDGES)
    for stop_index in range(STOPS):
        offset = (neg_owner[stop_index] * PART_ROWS).astype(jnp.int32)
        owner_rows = lax.dynamic_slice_in_dim(embeddings, offset, PART_ROWS, 0)
        negatives = jnp.take(owner_rows, neg_ids[stop_index], axis=0)
        relation_row = relation[stop_index]

        def one_block(inputs, stop_index=stop_index, negatives=negatives, relation_row=relation_row):
            block, head_index, context_index = inputs
            home_rows = lax.dynamic_slice_in_dim(embeddings, (block * PART_ROWS).astype(jnp.int32), PART_ROWS, 0)
            source = (((block - stop_index - 1) % N_BLK) * PART_ROWS).astype(jnp.int32)
            visitor = lax.dynamic_slice_in_dim(embeddings, source, PART_ROWS, 0)
            return stop_terms(home_rows, visitor, negatives, relation_row, head_index, context_index, weight)

        blocks = jnp.arange(N_BLK, dtype=jnp.int32)
        head_parts, context_parts = lax.map(one_block, (blocks, head_blocks[stop_index], context_blocks[stop_index]))
        gradient = gradient + head_parts.reshape(ENT, D)
        gradient = gradient + jnp.roll(context_parts, -(stop_index + 1), axis=0).reshape(ENT, D)
    return gradient
```

```python
import functools

import jax
import jax.numpy as jnp
from jax import lax
from jax.experimental import pallas as pl
from jax.experimental.pallas import tpu as pltpu
from jax.sharding import PartitionSpec as P

MESH = pl.DeviceIdType.MESH
F32 = jnp.float32
BF16 = jnp.bfloat16


def column_of(row):
    wide = jnp.broadcast_to(row.astype(F32), (8, row.shape[1]))
    return jnp.transpose(wide)[:, :1]


def by_edge(row, rows):
    column = column_of(row)
    lanes = lax.broadcasted_iota(jnp.int32, (row.shape[1], rows), 1).astype(F32)
    return jnp.where(column == lanes, 1.0, 0.0).astype(BF16)


def by_entity(row, rows, value):
    sublanes = lax.broadcasted_iota(jnp.int32, (rows, row.shape[1]), 0)
    return jnp.where(row == sublanes, value, 0.0).astype(BF16)


def kernel(
    n_blk, n_rep, weight,
    owner_ref, emb_ref, rel_ref, ids_ref, neg_ids_ref, out_ref,
    parts, idz, idn, mine, his, ctx, part_dot, pos_grad, pos_in, neg_cut, neg, pulled, spread, give, take,
    wide, rel_cols, rel_stop, ag_send, ag_recv, fw_send, fw_recv, idz_send, idz_recv, idn_send, idn_recv,
    dot_send, dot_recv, pg_send, pg_recv, neg_send, neg_recv, sib_send, sib_recv, rs_send, rs_recv,
):
    b, z = lax.axis_index("blk"), lax.axis_index("rep")
    rows = emb_ref.shape[0]
    stops = rel_ref.shape[0]
    edges = ids_ref.shape[1]
    width = out_ref.shape[1]
    negs = neg_ids_ref.shape[1]
    half = negs // 2
    core = lax.rem(b, 2)
    sibling = b + 1 - 2 * core
    cols = pl.ds(pl.multiple_of(z * width, width), width)

    def plane(j):
        return lax.rem(b + j + n_blk, n_blk)

    def column_peer(j):
        return lax.rem(z + j + n_rep, n_rep)

    def remote(src, dst, send, recv, at_blk, at_rep):
        return pltpu.make_async_remote_copy(
            src_ref=src, dst_ref=dst, send_sem=send, recv_sem=recv,
            device_id=(at_blk, at_rep), device_id_type=MESH,
        )

    barrier = pltpu.get_barrier_semaphore()
    for j in range(1, n_blk):
        pl.semaphore_signal(barrier, inc=1, device_id=(plane(j), z), device_id_type=MESH)
    for j in range(1, n_rep):
        pl.semaphore_signal(barrier, inc=1, device_id=(b, column_peer(j)), device_id_type=MESH)
    parts[b] = emb_ref[:, cols]
    rel_cols[...] = rel_ref[:, cols]
    own_relation = rel_ref[pl.ds(z, 1), :]
    for r in range(n_rep):
        rel_stop[r] = own_relation[:, r * width : (r + 1) * width]
    idz[z] = ids_ref[...]
    pl.semaphore_wait(barrier, n_blk - 1 + n_rep - 1)

    idz_copies = [
        remote(idz.at[z], idz.at[z], idz_send.at[j], idz_recv.at[j], b, column_peer(j))
        for j in range(1, n_rep)
    ]
    for copy in idz_copies:
        copy.start()
    jumps = list(range(2, n_blk, 2))
    ag_copies = [
        remote(parts.at[b], parts.at[b], ag_send.at[i], ag_recv.at[i], plane(j), z)
        for i, j in enumerate(jumps)
    ]
    for copy in ag_copies:
        copy.start()
    own_fw = remote(parts.at[b], parts.at[b], fw_send.at[len(jumps)], fw_recv.at[len(jumps)], sibling, z)
    own_fw.start()
    for copy in idz_copies:
        copy.wait()
    idn_copies = [
        remote(idz, idn.at[k - 1], idn_send.at[k - 1], idn_recv.at[k - 1], plane(-k), z)
        for k in range(1, stops + 1)
    ]
    for copy in idn_copies:
        copy.start()

    def gather_home(t, carry):
        s, r = t // n_rep, lax.rem(t, n_rep)
        hot = by_edge(idz[r, pl.ds(s, 1), :], rows)
        picked = jnp.dot(hot, parts[b], preferred_element_type=F32)
        mine[t] = (picked * rel_cols[pl.ds(s, 1), :]).astype(BF16)
        return carry

    def gather_wide(r, carry):
        hot = by_edge(idz[r, pl.ds(z, 1), :], rows)
        picked = jnp.dot(hot, emb_ref[...], preferred_element_type=F32)
        wide[r] = (picked * rel_ref[pl.ds(z, 1), :]).astype(BF16)
        return carry

    lax.fori_loop(0, n_rep, gather_wide, 0)

    fw_copies = []
    for i, j in enumerate(jumps):
        ag_copies[i].wait()
        source = plane(-j)
        copy = remote(parts.at[source], parts.at[source], fw_send.at[i], fw_recv.at[i], sibling, z)
        copy.start()
        fw_copies.append(copy)
    lax.fori_loop(0, stops * n_rep, gather_home, 0)
    for copy in fw_copies + [own_fw]:
        copy.wait()

    lower = pl.ds(pl.multiple_of(core * half, half), half)
    for s in range(stops):
        ids_row = jnp.where(core == 0, neg_ids_ref[s : s + 1, :half], neg_ids_ref[s : s + 1, half:])
        hot = by_edge(ids_row, rows)
        neg_cut[s] = jnp.dot(hot, parts[owner_ref[s]], preferred_element_type=F32).astype(BF16)
    neg_copies = [
        remote(neg_cut.at[column_peer(j)], neg.at[lower, cols], neg_send.at[j], neg_recv.at[j], b, column_peer(j))
        for j in range(1, n_rep)
    ]
    for copy in neg_copies:
        copy.start()
    neg[lower, cols] = neg_cut[z]

    def gather_context(t, carry):
        s, r = t // n_rep, lax.rem(t, n_rep)
        hot = by_edge(idz[r, pl.ds(stops + s, 1), :], rows)
        rows_in = jnp.dot(hot, parts[lax.rem(b - s - 1 + n_blk, n_blk)], preferred_element_type=F32)
        ctx[t] = rows_in.astype(BF16)
        product = mine[t].astype(F32) * rows_in
        part_dot[z, pl.ds(t, 1), :] = jnp.sum(jnp.transpose(product), axis=0, keepdims=True)
        return carry

    lax.fori_loop(0, stops * n_rep, gather_context, 0)
    dot_copies = [
        remote(part_dot.at[z], part_dot.at[z], dot_send.at[j], dot_recv.at[j], b, column_peer(j))
        for j in range(1, n_rep)
    ]
    for copy in dot_copies:
        copy.start()

    for copy in idn_copies:
        copy.wait()

    def gather_incoming(t, carry):
        s, r = t // n_rep, lax.rem(t, n_rep)
        hot = by_edge(idn[s, r, pl.ds(s, 1), :], rows)
        picked = jnp.dot(hot, parts[lax.rem(b + s + 1, n_blk)], preferred_element_type=F32)
        his[t] = (picked * rel_cols[pl.ds(s, 1), :]).astype(BF16)
        return carry

    for copy in neg_copies:
        copy.wait()
    sib_copy = remote(neg.at[lower, :], neg.at[lower, :], sib_send, sib_recv, sibling, z)
    sib_copy.start()
    for copy in dot_copies:
        copy.wait()
    positive = part_dot[0]
    for r in range(1, n_rep):
        positive = positive + part_dot[r]
    pos_grad[...] = -jax.nn.sigmoid(-positive)
    pg_copies = [
        remote(pos_grad, pos_in.at[k - 1], pg_send.at[k - 1], pg_recv.at[k - 1], plane(-k), z)
        for k in range(1, stops + 1)
    ]
    for copy in pg_copies:
        copy.start()
    sib_copy.wait()

    def negatives(r, carry):
        scores = lax.dot_general(
            wide[r], neg[...], (((1,), (1,)), ((), ())), preferred_element_type=F32
        )
        neg_grad = (weight * jax.nn.sigmoid(scores)).astype(BF16)
        at = pl.ds(pl.multiple_of(r * edges, edges), edges)
        pulled[at, :] = jnp.dot(neg_grad, neg[...], preferred_element_type=F32).astype(BF16)
        spread[:, at] = by_entity(idz[r, pl.ds(z, 1), :], rows, 1.0)
        return carry

    lax.fori_loop(0, n_rep, negatives, 0)
    rs_copies = []
    for j in list(range(1, n_rep)) + [0]:
        to = column_peer(j)
        there = pl.ds(pl.multiple_of(to * width, width), width)
        summed = jnp.dot(spread[...], pulled[:, there], preferred_element_type=F32)
        summed = summed * rel_stop[to]
        if j == 0:
            out_ref[...] = summed
        else:
            give[j - 1] = summed.astype(BF16)
            copy = remote(give.at[j - 1], take.at[j - 1], rs_send.at[j], rs_recv.at[j], b, to)
            copy.start()
            rs_copies.append(copy)
    lax.fori_loop(0, stops * n_rep, gather_incoming, 0)

    def scatter_home(s, carry):
        total = jnp.zeros((rows, width), F32)
        for r in range(n_rep):
            t = s * n_rep + r
            hot = by_entity(idz[r, pl.ds(s, 1), :], rows, pos_grad[pl.ds(t, 1), :])
            total = total + jnp.dot(hot, ctx[t], preferred_element_type=F32)
        out_ref[...] += total * rel_cols[pl.ds(s, 1), :]
        return carry

    lax.fori_loop(0, stops, scatter_home, 0)
    for copy in pg_copies:
        copy.wait()

    def scatter_incoming(s, carry):
        total = jnp.zeros((rows, width), F32)
        for r in range(n_rep):
            t = s * n_rep + r
            hot = by_entity(idn[s, r, pl.ds(stops + s, 1), :], rows, pos_in[s, pl.ds(t, 1), :])
            total = total + jnp.dot(hot, his[t], preferred_element_type=F32)
        out_ref[...] += total
        return carry

    lax.fori_loop(0, stops, scatter_incoming, 0)
    for copy in rs_copies:
        copy.wait()
    for j in range(n_rep - 1):
        out_ref[...] += take[j].astype(F32)


def fused(n_blk, n_rep, embeddings, relation, head_ids, context_ids, neg_owner, neg_ids):
    rows, dim = embeddings.shape
    stops, edges = head_ids.shape
    negs = neg_ids.shape[1]
    width = dim // n_rep
    ids = jnp.concatenate([head_ids, context_ids], axis=0)
    blocks = stops * n_rep
    vmem = pl.BlockSpec(memory_space=pltpu.VMEM)
    dma = pltpu.SemaphoreType.DMA
    return pl.pallas_call(
        functools.partial(kernel, n_blk, n_rep, 4.0 / negs),
        out_shape=jax.ShapeDtypeStruct((rows, width), F32),
        in_specs=[pl.BlockSpec(memory_space=pltpu.SMEM)] + [vmem] * 4,
        out_specs=vmem,
        scratch_shapes=[
            pltpu.VMEM((n_blk, rows, width), BF16),
            pltpu.VMEM((n_rep, 2 * stops, edges), jnp.int32),
            pltpu.VMEM((stops, n_rep, 2 * stops, edges), jnp.int32),
            pltpu.VMEM((blocks, edges, width), BF16),
            pltpu.VMEM((blocks, edges, width), BF16),
            pltpu.VMEM((blocks, edges, width), BF16),
            pltpu.VMEM((n_rep, blocks, edges), F32),
            pltpu.VMEM((blocks, edges), F32),
            pltpu.VMEM((stops, blocks, edges), F32),
            pltpu.VMEM((stops, negs // 2, width), BF16),
            pltpu.VMEM((negs, dim), BF16),
            pltpu.VMEM((n_rep * edges, dim), BF16),
            pltpu.VMEM((rows, n_rep * edges), BF16),
            pltpu.VMEM((n_rep - 1, rows, width), BF16),
            pltpu.VMEM((n_rep - 1, rows, width), BF16),
            pltpu.VMEM((n_rep, edges, dim), BF16),
            pltpu.VMEM((stops, width), F32),
            pltpu.VMEM((n_rep, 1, width), F32),
            dma((n_blk // 2,)), dma((n_blk // 2,)), dma((n_blk // 2,)), dma((n_blk // 2,)),
            dma((n_rep,)), dma((n_rep,)), dma((stops,)), dma((stops,)),
            dma((n_rep,)), dma((n_rep,)), dma((stops,)), dma((stops,)),
            dma((n_rep,)), dma((n_rep,)), dma, dma, dma((n_rep,)), dma((n_rep,)),
        ],
        compiler_params=pltpu.CompilerParams(
            collective_id=0, has_side_effects=True, vmem_limit_bytes=48 * 1024 * 1024
        ),
    )(neg_owner, embeddings, relation, ids, neg_ids)


def shifted(shard, axis, by):
    peers = lax.axis_size(axis)
    return lax.ppermute(shard, axis, [(i, (i + by) % peers) for i in range(peers)])


def broadcast(value, axis, source):
    kept = jnp.where(lax.axis_index(axis) == source, value, 0).astype(value.dtype)
    return lax.psum(kept, axis)


def stop_terms(home_rows, visitor, negatives, relation_row, head_index, context_index, weight):
    head_rows = jnp.take(home_rows, head_index, axis=0)
    context_rows = jnp.take(visitor, context_index, axis=0)
    weighted = (head_rows.astype(jnp.float32) * relation_row).astype(jnp.bfloat16)
    positive = jnp.sum(weighted.astype(jnp.float32) * context_rows.astype(jnp.float32), axis=1)
    scores = lax.dot_general(
        weighted, negatives, (((1,), (1,)), ((), ())), preferred_element_type=jnp.float32
    )
    pos_grad = -jax.nn.sigmoid(-positive)
    neg_grad = (weight * jax.nn.sigmoid(scores)).astype(jnp.bfloat16)
    pulled = jnp.dot(neg_grad, negatives, preferred_element_type=jnp.float32)
    head_terms = relation_row * (pos_grad[:, None] * context_rows.astype(jnp.float32) + pulled)
    context_terms = pos_grad[:, None] * weighted.astype(jnp.float32)
    empty = jnp.zeros((home_rows.shape[0], home_rows.shape[1]), jnp.float32)
    return (empty.at[head_index].add(head_terms), empty.at[context_index].add(context_terms))


def by_collectives(embeddings, relation, head_ids, context_ids, neg_owner, neg_ids):
    weight = 4.0 / neg_ids.shape[1]
    stop_count = head_ids.shape[0]
    visitor = embeddings
    head_total = jnp.zeros(embeddings.shape, jnp.float32)
    returned = jnp.zeros(embeddings.shape, jnp.float32)
    for stop_index in range(stop_count):
        visitor = shifted(visitor, "blk", 1)
        owner = neg_owner[stop_index]
        picked = jnp.take(embeddings, neg_ids[stop_index], axis=0)
        negatives = broadcast(picked, "blk", owner)
        head_part, context_part = stop_terms(
            embeddings,
            visitor,
            negatives,
            relation[stop_index],
            head_ids[stop_index],
            context_ids[stop_index],
            weight,
        )
        head_total = head_total + head_part
        returned = returned + shifted(
            context_part.astype(jnp.bfloat16), "blk", -(stop_index + 1)
        ).astype(context_part.dtype)
    combined = head_total + returned
    return lax.psum_scatter(combined, "rep", scatter_dimension=1, tiled=True)


def per_device(n_blk, n_rep, embeddings, relation, head_ids, context_ids, neg_owner, neg_ids):
    rows, dim = embeddings.shape
    stops = head_ids.shape[0]
    fits = n_blk * rows * (dim // n_rep) * 2 <= 8 * 1024 * 1024
    if fits and n_rep == stops and n_blk > stops and n_blk % 2 == 0:
        return fused(n_blk, n_rep, embeddings, relation, head_ids, context_ids, neg_owner, neg_ids)
    return by_collectives(embeddings, relation, head_ids, context_ids, neg_owner, neg_ids)


def solution(mesh):
    in_specs = (P("blk", None), P(), P(None, ("blk", "rep")), P(None, ("blk", "rep")), P(), P())
    out_specs = P("blk", "rep")
    return jax.shard_map(
        functools.partial(per_device, mesh.shape["blk"], mesh.shape["rep"]), mesh=mesh, in_specs=in_specs, out_specs=out_specs, check_vma=False
    )
```

```python
import functools

import jax
import jax.numpy as jnp
from jax import lax
from jax.experimental import pallas as pl
from jax.experimental.pallas import tpu as pltpu
from jax.sharding import PartitionSpec as P

MESH = pl.DeviceIdType.MESH
F32 = jnp.float32
BF16 = jnp.bfloat16


def column_of(row):
    wide = jnp.broadcast_to(row.astype(F32), (8, row.shape[1]))
    return jnp.transpose(wide)[:, :1]


def by_edge(row, rows):
    column = column_of(row)
    lanes = lax.broadcasted_iota(jnp.int32, (row.shape[1], rows), 1).astype(F32)
    return jnp.where(column == lanes, 1.0, 0.0).astype(BF16)


def by_entity(row, rows, value):
    sublanes = lax.broadcasted_iota(jnp.int32, (rows, row.shape[1]), 0)
    return jnp.where(row == sublanes, value, 0.0).astype(BF16)


def kernel(
    n_blk, n_rep, weight,
    owner_ref, emb_hbm, rel_hbm, head_hbm, ctx_hbm, negid_hbm, out_ref,
    emb, rel, neg_ids, load_sem,
    parts, idz, idn, mine, his, ctx, part_dot, pos_grad, pos_in, neg_hot, neg_cut, neg, pulled, spread, give, take,
    wide, rel_wide, ag_send, ag_recv, fw_send, fw_recv, idz_send, idz_recv, idn_send, idn_recv,
    dot_send, dot_recv, pg_send, pg_recv, neg_send, neg_recv, sib_send, sib_recv, rs_send, rs_recv,
):
    b, z = lax.axis_index("blk"), lax.axis_index("rep")
    rows = emb.shape[0]
    stops = rel.shape[0]
    edges = idz.shape[2]
    width = out_ref.shape[1]
    half = neg_ids.shape[1] // 2
    core = lax.rem(b, 2)
    sibling = b + 1 - 2 * core
    cols = pl.ds(pl.multiple_of(z * width, width), width)
    inner = (z >= 1) & (z <= 2)
    first_stop = jnp.where(z == 2, 2, 0)

    def plane(j):
        return lax.rem(b + j + n_blk, n_blk)

    def column_peer(j):
        return lax.rem(z + j + n_rep, n_rep)

    def remote(src, dst, send, recv, at_blk, at_rep):
        return pltpu.make_async_remote_copy(
            src_ref=src, dst_ref=dst, send_sem=send, recv_sem=recv,
            device_id=(at_blk, at_rep), device_id_type=MESH,
        )

    barrier = pltpu.get_barrier_semaphore()
    for j in range(1, n_blk):
        pl.semaphore_signal(barrier, inc=1, device_id=(plane(j), z), device_id_type=MESH)
    for j in range(1, n_rep):
        pl.semaphore_signal(barrier, inc=1, device_id=(b, column_peer(j)), device_id_type=MESH)
    loads = [
        pltpu.make_async_copy(emb_hbm, emb, load_sem.at[0]),
        pltpu.make_async_copy(head_hbm, idz.at[z, pl.ds(0, stops)], load_sem.at[1]),
        pltpu.make_async_copy(ctx_hbm, idz.at[z, pl.ds(stops, stops)], load_sem.at[2]),
        pltpu.make_async_copy(rel_hbm, rel, load_sem.at[3]),
        pltpu.make_async_copy(negid_hbm, neg_ids, load_sem.at[4]),
    ]
    for copy in loads:
        copy.start()
    for copy in loads[1:]:
        copy.wait()
    loads[0].wait()
    parts[b] = jnp.transpose(emb[:, cols])
    pl.semaphore_wait(barrier, n_blk - 1 + n_rep - 1)

    jumps = list(range(2, n_blk, 2))
    ag_copies = [
        remote(parts.at[b], parts.at[b], ag_send.at[i], ag_recv.at[i], plane(j), z)
        for i, j in enumerate(jumps)
    ]
    for copy in ag_copies:
        copy.start()
    own_fw = remote(parts.at[b], parts.at[b], fw_send.at[len(jumps)], fw_recv.at[len(jumps)], sibling, z)
    own_fw.start()
    idz_copies = [
        remote(idz.at[z], idz.at[z], idz_send.at[j], idz_recv.at[j], b, column_peer(j))
        for j in range(1, n_rep)
    ]
    for copy in idz_copies:
        copy.start()

    rel_cols = rel[:, cols]
    for s in range(stops):
        rel_wide[s] = jnp.broadcast_to(column_of(rel_cols[s : s + 1, :]), (width, edges))
    for s in range(stops):
        ids_row = jnp.where(core == 0, neg_ids[s : s + 1, :half], neg_ids[s : s + 1, half:])
        neg_hot[s] = by_edge(ids_row, rows)

    for copy in idz_copies:
        copy.wait()
    idn_copies = [
        remote(idz, idn.at[k - 1], idn_send.at[k - 1], idn_recv.at[k - 1], plane(-k), z)
        for k in range(1, stops + 1)
    ]
    for copy in idn_copies:
        copy.start()

    def gather_wide(i, carry):
        s = first_stop + i
        for r in range(n_rep):
            at = pl.ds(pl.multiple_of((i * n_rep + r) * edges, edges), edges)
            ids_row = idz[r, pl.ds(s, 1), :]
            picked = jnp.dot(by_edge(ids_row, rows), emb[...], preferred_element_type=F32)
            wide[at, :] = (picked * rel[pl.ds(s, 1), :]).astype(BF16)
            spread[:, at] = by_entity(ids_row, rows, 1.0)
        return carry

    @pl.when(inner)
    def _():
        lax.fori_loop(0, 2, gather_wide, 0)

    fw_copies = []
    for i, j in enumerate(jumps):
        ag_copies[i].wait()
        source = plane(-j)
        copy = remote(parts.at[source], parts.at[source], fw_send.at[i], fw_recv.at[i], sibling, z)
        copy.start()
        fw_copies.append(copy)

    def gather_home(s, carry):
        for r in range(n_rep):
            hot = by_entity(idz[r, pl.ds(s, 1), :], rows, 1.0)
            picked = jnp.dot(parts[b], hot, preferred_element_type=F32)
            mine[s * n_rep + r] = (picked * rel_wide[s]).astype(BF16)
        return carry

    lax.fori_loop(0, stops, gather_home, 0)
    for copy in fw_copies + [own_fw]:
        copy.wait()

    lower = pl.ds(pl.multiple_of(core * half, half), half)
    by_row = (((1,), (1,)), ((), ()))
    neg_copies = []
    for s in range(stops):
        cut = lax.dot_general(neg_hot[s], parts[owner_ref[s]], by_row, preferred_element_type=F32)
        neg_cut[s] = cut.astype(BF16)
        to = 1 + s // 2
        copy = remote(
            neg_cut.at[s], neg.at[s % 2, lower, cols], neg_send.at[s], neg_recv.at[s % 2, z], b, to
        )
        neg_copies.append((to, copy))

        @pl.when(z != to)
        def _():
            copy.start()

        @pl.when(z == to)
        def _():
            neg[s % 2, lower, cols] = neg_cut[s]

    def gather_context(s, carry):
        source = lax.rem(b - s - 1 + n_blk, n_blk)
        for r in range(n_rep):
            t = s * n_rep + r
            hot = by_entity(idz[r, pl.ds(stops + s, 1), :], rows, 1.0)
            rows_in = jnp.dot(parts[source], hot, preferred_element_type=F32)
            ctx[t] = rows_in.astype(BF16)
            product = mine[t].astype(F32) * rows_in
            part_dot[z, pl.ds(t, 1), :] = jnp.sum(product, axis=0, keepdims=True)
        return carry

    lax.fori_loop(0, stops, gather_context, 0)
    dot_copies = [
        remote(part_dot.at[z], part_dot.at[z], dot_send.at[j], dot_recv.at[j], b, column_peer(j))
        for j in range(1, n_rep)
    ]
    for copy in dot_copies:
        copy.start()
    for copy in idn_copies:
        copy.wait()

    def gather_incoming(s, carry):
        source = lax.rem(b + s + 1, n_blk)
        for r in range(n_rep):
            hot = by_entity(idn[s, r, pl.ds(s, 1), :], rows, 1.0)
            picked = jnp.dot(parts[source], hot, preferred_element_type=F32)
            his[s * n_rep + r] = (picked * rel_wide[s]).astype(BF16)
        return carry

    for to, copy in neg_copies:

        @pl.when(z != to)
        def _():
            copy.wait_send()

    sib_copy = remote(neg.at[:, lower, :], neg.at[:, lower, :], sib_send, sib_recv, sibling, z)

    @pl.when(inner)
    def _():
        for i in range(2):
            for source in range(n_rep):

                @pl.when(z != source)
                def _():
                    there = pl.ds(source * width, width)
                    remote(
                        neg_cut.at[i], neg.at[i, lower, there], neg_send.at[i], neg_recv.at[i, source], b, source
                    ).wait_recv()

        sib_copy.start()

    for copy in dot_copies:
        copy.wait()
    positive = part_dot[0]
    for r in range(1, n_rep):
        positive = positive + part_dot[r]
    pos_grad[...] = -jax.nn.sigmoid(-positive)
    pg_copies = [
        remote(pos_grad, pos_in.at[k - 1], pg_send.at[k - 1], pg_recv.at[k - 1], plane(-k), z)
        for k in range(1, stops + 1)
    ]
    for copy in pg_copies:
        copy.start()

    def negatives(t, carry):
        i = t // n_rep
        at = pl.ds(pl.multiple_of(t * edges, edges), edges)
        scores = lax.dot_general(wide[at, :], neg[i], by_row, preferred_element_type=F32)
        neg_grad = (weight * jax.nn.sigmoid(scores)).astype(BF16)
        pull = jnp.dot(neg_grad, neg[i], preferred_element_type=F32)
        pulled[at, :] = (pull * rel[pl.ds(first_stop + i, 1), :]).astype(BF16)
        return carry

    def rs_copy(to):
        return remote(give.at[to], take.at[z - 1], rs_send.at[to], rs_recv.at[z - 1], b, to)

    @pl.when(inner)
    def _():
        sib_copy.wait()
        lax.fori_loop(0, 2 * n_rep, negatives, 0)
        for to in (0, 3, 1, 2):
            there = pl.ds(to * width, width)
            summed = jnp.dot(spread[...], pulled[:, there], preferred_element_type=F32)
            give[to] = summed.astype(BF16)

            @pl.when(z != to)
            def _():
                rs_copy(to).start()

            @pl.when(z == to)
            def _():
                out_ref[...] = summed

    @pl.when(jnp.logical_not(inner))
    def _():
        out_ref[...] = jnp.zeros_like(out_ref)

    lax.fori_loop(0, stops, gather_incoming, 0)

    def scatter_home(s, carry):
        total = jnp.zeros((rows, width), F32)
        for r in range(n_rep):
            t = s * n_rep + r
            hot = by_entity(idz[r, pl.ds(s, 1), :], rows, pos_grad[pl.ds(t, 1), :])
            rows_in = (ctx[t].astype(F32) * rel_wide[s]).astype(BF16)
            total = total + lax.dot_general(hot, rows_in, by_row, preferred_element_type=F32)
        out_ref[...] += total
        return carry

    lax.fori_loop(0, stops, scatter_home, 0)
    for copy in pg_copies:
        copy.wait()

    def scatter_incoming(s, carry):
        total = jnp.zeros((rows, width), F32)
        for r in range(n_rep):
            t = s * n_rep + r
            hot = by_entity(idn[s, r, pl.ds(stops + s, 1), :], rows, pos_in[s, pl.ds(t, 1), :])
            total = total + lax.dot_general(hot, his[t], by_row, preferred_element_type=F32)
        out_ref[...] += total
        return carry

    lax.fori_loop(0, stops, scatter_incoming, 0)
    for source in (1, 2):

        @pl.when(z != source)
        def _():
            remote(
                give.at[0], take.at[source - 1], rs_send.at[0], rs_recv.at[source - 1], b, source
            ).wait_recv()
            out_ref[...] += take[source - 1].astype(F32)

    @pl.when(inner)
    def _():
        for to in range(n_rep):

            @pl.when(z != to)
            def _():
                rs_copy(to).wait_send()


def fused(n_blk, n_rep, embeddings, relation, head_ids, context_ids, neg_owner, neg_ids):
    rows, dim = embeddings.shape
    stops, edges = head_ids.shape
    negs = neg_ids.shape[1]
    width = dim // n_rep
    blocks = stops * n_rep
    hbm = pl.BlockSpec(memory_space=pl.ANY)
    dma = pltpu.SemaphoreType.DMA
    return pl.pallas_call(
        functools.partial(kernel, n_blk, n_rep, 4.0 / negs),
        out_shape=jax.ShapeDtypeStruct((rows, width), F32),
        in_specs=[pl.BlockSpec(memory_space=pltpu.SMEM)] + [hbm] * 5,
        out_specs=pl.BlockSpec(memory_space=pltpu.VMEM),
        scratch_shapes=[
            pltpu.VMEM((rows, dim), BF16),
            pltpu.VMEM((stops, dim), F32),
            pltpu.VMEM((stops, negs), jnp.int32),
            dma((5,)),
            pltpu.VMEM((n_blk, width, rows), BF16),
            pltpu.VMEM((n_rep, 2 * stops, edges), jnp.int32),
            pltpu.VMEM((stops, n_rep, 2 * stops, edges), jnp.int32),
            pltpu.VMEM((blocks, width, edges), BF16),
            pltpu.VMEM((blocks, width, edges), BF16),
            pltpu.VMEM((blocks, width, edges), BF16),
            pltpu.VMEM((n_rep, blocks, edges), F32),
            pltpu.VMEM((blocks, edges), F32),
            pltpu.VMEM((stops, blocks, edges), F32),
            pltpu.VMEM((stops, negs // 2, rows), BF16),
            pltpu.VMEM((stops, negs // 2, width), BF16),
            pltpu.VMEM((2, negs, dim), BF16),
            pltpu.VMEM((2 * n_rep * edges, dim), BF16),
            pltpu.VMEM((rows, 2 * n_rep * edges), BF16),
            pltpu.VMEM((n_rep, rows, width), BF16),
            pltpu.VMEM((2, rows, width), BF16),
            pltpu.VMEM((2 * n_rep * edges, dim), BF16),
            pltpu.VMEM((stops, width, edges), F32),
            dma((n_blk // 2,)), dma((n_blk // 2,)), dma((n_blk // 2,)), dma((n_blk // 2,)),
            dma((n_rep,)), dma((n_rep,)), dma((stops,)), dma((stops,)),
            dma((n_rep,)), dma((n_rep,)), dma((stops,)), dma((stops,)),
            dma((stops,)), dma((2, n_rep)), dma, dma, dma((n_rep,)), dma((2,)),
        ],
        compiler_params=pltpu.CompilerParams(
            collective_id=0, has_side_effects=True, vmem_limit_bytes=52 * 1024 * 1024
        ),
    )(neg_owner, embeddings, relation, head_ids, context_ids, neg_ids)


def shifted(shard, axis, by):
    peers = lax.axis_size(axis)
    return lax.ppermute(shard, axis, [(i, (i + by) % peers) for i in range(peers)])


def broadcast(value, axis, source):
    kept = jnp.where(lax.axis_index(axis) == source, value, 0).astype(value.dtype)
    return lax.psum(kept, axis)


def stop_terms(home_rows, visitor, negatives, relation_row, head_index, context_index, weight):
    head_rows = jnp.take(home_rows, head_index, axis=0)
    context_rows = jnp.take(visitor, context_index, axis=0)
    weighted = (head_rows.astype(jnp.float32) * relation_row).astype(jnp.bfloat16)
    positive = jnp.sum(weighted.astype(jnp.float32) * context_rows.astype(jnp.float32), axis=1)
    scores = lax.dot_general(
        weighted, negatives, (((1,), (1,)), ((), ())), preferred_element_type=jnp.float32
    )
    pos_grad = -jax.nn.sigmoid(-positive)
    neg_grad = (weight * jax.nn.sigmoid(scores)).astype(jnp.bfloat16)
    pulled = jnp.dot(neg_grad, negatives, preferred_element_type=jnp.float32)
    head_terms = relation_row * (pos_grad[:, None] * context_rows.astype(jnp.float32) + pulled)
    context_terms = pos_grad[:, None] * weighted.astype(jnp.float32)
    empty = jnp.zeros((home_rows.shape[0], home_rows.shape[1]), jnp.float32)
    return (empty.at[head_index].add(head_terms), empty.at[context_index].add(context_terms))


def by_collectives(embeddings, relation, head_ids, context_ids, neg_owner, neg_ids):
    weight = 4.0 / neg_ids.shape[1]
    stop_count = head_ids.shape[0]
    visitor = embeddings
    head_total = jnp.zeros(embeddings.shape, jnp.float32)
    returned = jnp.zeros(embeddings.shape, jnp.float32)
    for stop_index in range(stop_count):
        visitor = shifted(visitor, "blk", 1)
        owner = neg_owner[stop_index]
        picked = jnp.take(embeddings, neg_ids[stop_index], axis=0)
        negatives = broadcast(picked, "blk", owner)
        head_part, context_part = stop_terms(
            embeddings,
            visitor,
            negatives,
            relation[stop_index],
            head_ids[stop_index],
            context_ids[stop_index],
            weight,
        )
        head_total = head_total + head_part
        returned = returned + shifted(
            context_part.astype(jnp.bfloat16), "blk", -(stop_index + 1)
        ).astype(context_part.dtype)
    combined = head_total + returned
    return lax.psum_scatter(combined, "rep", scatter_dimension=1, tiled=True)


def per_device(n_blk, n_rep, embeddings, relation, head_ids, context_ids, neg_owner, neg_ids):
    rows, dim = embeddings.shape
    stops = head_ids.shape[0]
    fits = n_blk * rows * (dim // n_rep) * 2 <= 8 * 1024 * 1024
    if fits and n_rep == stops == 4 and n_blk > stops and n_blk % 2 == 0:
        return fused(n_blk, n_rep, embeddings, relation, head_ids, context_ids, neg_owner, neg_ids)
    return by_collectives(embeddings, relation, head_ids, context_ids, neg_owner, neg_ids)


def solution(mesh):
    in_specs = (P("blk", None), P(), P(None, ("blk", "rep")), P(None, ("blk", "rep")), P(), P())
    out_specs = P("blk", "rep")
    return jax.shard_map(
        functools.partial(per_device, mesh.shape["blk"], mesh.shape["rep"]), mesh=mesh, in_specs=in_specs, out_specs=out_specs, check_vma=False
    )
```

```python
import functools

import jax
import jax.numpy as jnp
from jax import lax
from jax.experimental import pallas as pl
from jax.experimental.pallas import tpu as pltpu
from jax.sharding import PartitionSpec as P

MESH = pl.DeviceIdType.MESH
F32 = jnp.float32
BF16 = jnp.bfloat16


def column_of(row):
    wide = jnp.broadcast_to(row.astype(F32), (8, row.shape[1]))
    return jnp.transpose(wide)[:, :1]


def by_edge(row, rows):
    column = column_of(row)
    lanes = lax.broadcasted_iota(jnp.int32, (row.shape[1], rows), 1).astype(F32)
    return jnp.where(column == lanes, 1.0, 0.0).astype(BF16)


def by_entity(row, rows, value):
    sublanes = lax.broadcasted_iota(jnp.int32, (rows, row.shape[1]), 0)
    return jnp.where(row == sublanes, value, 0.0).astype(BF16)


def kernel(
    n_blk, n_rep, weight,
    owner_ref, emb_hbm, rel_hbm, head_hbm, ctx_hbm, negid_hbm, out_ref,
    emb, rel, neg_ids, load_sem,
    parts, idz, idn, mine, his, ctx, part_dot, pos_grad, pos_in, neg_hot, neg_cut, neg, pulled, spread, give, take,
    wide, rel_wide, ag_send, ag_recv, fw_send, fw_recv, idz_send, idz_recv, idn_send, idn_recv,
    dot_send, dot_recv, pg_send, pg_recv, neg_send, neg_recv, sib_send, sib_recv, rs_send, rs_recv,
):
    b, z = lax.axis_index("blk"), lax.axis_index("rep")
    rows = emb.shape[0]
    stops = rel.shape[0]
    edges = idz.shape[2]
    width = out_ref.shape[1]
    half = neg_ids.shape[1] // 2
    core = lax.rem(b, 2)
    sibling = b + 1 - 2 * core
    cols = pl.ds(pl.multiple_of(z * width, width), width)
    inner = (z >= 1) & (z <= 2)
    first_stop = jnp.where(z == 2, 2, 0)

    def plane(j):
        return lax.rem(b + j + n_blk, n_blk)

    def column_peer(j):
        return lax.rem(z + j + n_rep, n_rep)

    def remote(src, dst, send, recv, at_blk, at_rep):
        return pltpu.make_async_remote_copy(
            src_ref=src, dst_ref=dst, send_sem=send, recv_sem=recv,
            device_id=(at_blk, at_rep), device_id_type=MESH,
        )

    barrier = pltpu.get_barrier_semaphore()
    for j in range(1, n_blk):
        pl.semaphore_signal(barrier, inc=1, device_id=(plane(j), z), device_id_type=MESH)
    for j in range(1, n_rep):
        pl.semaphore_signal(barrier, inc=1, device_id=(b, column_peer(j)), device_id_type=MESH)
    loads = [
        pltpu.make_async_copy(emb_hbm, emb, load_sem.at[0]),
        pltpu.make_async_copy(head_hbm, idz.at[z, pl.ds(0, stops)], load_sem.at[1]),
        pltpu.make_async_copy(ctx_hbm, idz.at[z, pl.ds(stops, stops)], load_sem.at[2]),
        pltpu.make_async_copy(rel_hbm, rel, load_sem.at[3]),
        pltpu.make_async_copy(negid_hbm, neg_ids, load_sem.at[4]),
    ]
    for copy in loads:
        copy.start()
    for copy in loads[1:]:
        copy.wait()
    loads[0].wait()
    parts[b] = jnp.transpose(emb[:, cols])
    pl.semaphore_wait(barrier, n_blk - 1 + n_rep - 1)

    jumps = list(range(2, n_blk, 2))
    ag_copies = [
        remote(parts.at[b], parts.at[b], ag_send.at[i], ag_recv.at[i], plane(j), z)
        for i, j in enumerate(jumps)
    ]
    for copy in ag_copies:
        copy.start()
    own_fw = remote(parts.at[b], parts.at[b], fw_send.at[len(jumps)], fw_recv.at[len(jumps)], sibling, z)
    own_fw.start()
    idz_copies = [
        remote(idz.at[z], idz.at[z], idz_send.at[j], idz_recv.at[j], b, column_peer(j))
        for j in range(1, n_rep)
    ]
    for copy in idz_copies:
        copy.start()

    rel_cols = rel[:, cols]
    for s in range(stops):
        rel_wide[s] = jnp.broadcast_to(column_of(rel_cols[s : s + 1, :]), (width, edges))
    for s in range(stops):
        ids_row = jnp.where(core == 0, neg_ids[s : s + 1, :half], neg_ids[s : s + 1, half:])
        neg_hot[s] = by_edge(ids_row, rows)

    for copy in idz_copies:
        copy.wait()
    idn_copies = [
        remote(idz, idn.at[k - 1], idn_send.at[k - 1], idn_recv.at[k - 1], plane(-k), z)
        for k in range(1, stops + 1)
    ]
    for copy in idn_copies:
        copy.start()

    def gather_wide(i, carry):
        s = first_stop + i
        for r in range(n_rep):
            at = pl.ds(pl.multiple_of((i * n_rep + r) * edges, edges), edges)
            ids_row = idz[r, pl.ds(s, 1), :]
            picked = jnp.dot(by_edge(ids_row, rows), emb[...], preferred_element_type=F32)
            wide[at, :] = (picked * rel[pl.ds(s, 1), :]).astype(BF16)
            spread[:, at] = by_entity(ids_row, rows, 1.0)
        return carry

    @pl.when(inner)
    def _():
        lax.fori_loop(0, 2, gather_wide, 0)

    fw_copies = []
    for i, j in enumerate(jumps):
        ag_copies[i].wait()
        source = plane(-j)
        copy = remote(parts.at[source], parts.at[source], fw_send.at[i], fw_recv.at[i], sibling, z)
        copy.start()
        fw_copies.append(copy)

    def gather_home(s, carry):
        for r in range(n_rep):
            hot = by_entity(idz[r, pl.ds(s, 1), :], rows, 1.0)
            picked = jnp.dot(parts[b], hot, preferred_element_type=F32)
            mine[s * n_rep + r] = (picked * rel_wide[s]).astype(BF16)
        return carry

    lax.fori_loop(0, stops, gather_home, 0)
    for copy in fw_copies + [own_fw]:
        copy.wait()

    lower = pl.ds(pl.multiple_of(core * half, half), half)
    by_row = (((1,), (1,)), ((), ()))
    neg_copies = []
    for s in range(stops):
        cut = lax.dot_general(neg_hot[s], parts[owner_ref[s]], by_row, preferred_element_type=F32)
        neg_cut[s] = cut.astype(BF16)
        to = 1 + s // 2
        copy = remote(
            neg_cut.at[s], neg.at[s % 2, lower, cols], neg_send.at[s], neg_recv.at[s % 2, z], b, to
        )
        neg_copies.append((to, copy))

        @pl.when(z != to)
        def _():
            copy.start()

        @pl.when(z == to)
        def _():
            neg[s % 2, lower, cols] = neg_cut[s]

    def gather_context(s, carry):
        source = lax.rem(b - s - 1 + n_blk, n_blk)
        for r in range(n_rep):
            t = s * n_rep + r
            hot = by_entity(idz[r, pl.ds(stops + s, 1), :], rows, 1.0)
            rows_in = jnp.dot(parts[source], hot, preferred_element_type=F32)
            ctx[t] = rows_in.astype(BF16)
            product = mine[t].astype(F32) * rows_in
            part_dot[z, pl.ds(t, 1), :] = jnp.sum(product, axis=0, keepdims=True)
        return carry

    lax.fori_loop(0, stops, gather_context, 0)
    dot_copies = [
        remote(part_dot.at[z], part_dot.at[z], dot_send.at[j], dot_recv.at[j], b, column_peer(j))
        for j in range(1, n_rep)
    ]
    for copy in dot_copies:
        copy.start()
    for copy in idn_copies:
        copy.wait()

    def gather_incoming(s, carry):
        source = lax.rem(b + s + 1, n_blk)
        for r in range(n_rep):
            hot = by_entity(idn[s, r, pl.ds(s, 1), :], rows, 1.0)
            picked = jnp.dot(parts[source], hot, preferred_element_type=F32)
            his[s * n_rep + r] = (picked * rel_wide[s]).astype(BF16)
        return carry

    for to, copy in neg_copies:

        @pl.when(z != to)
        def _():
            copy.wait_send()

    sib_copy = remote(neg.at[:, lower, :], neg.at[:, lower, :], sib_send, sib_recv, sibling, z)

    @pl.when(inner)
    def _():
        for i in range(2):
            for source in range(n_rep):

                @pl.when(z != source)
                def _():
                    there = pl.ds(source * width, width)
                    remote(
                        neg_cut.at[i], neg.at[i, lower, there], neg_send.at[i], neg_recv.at[i, source], b, source
                    ).wait_recv()

        sib_copy.start()

    for copy in dot_copies:
        copy.wait()
    positive = part_dot[0]
    for r in range(1, n_rep):
        positive = positive + part_dot[r]
    pos_grad[...] = -jax.nn.sigmoid(-positive)
    pg_copies = [
        remote(pos_grad, pos_in.at[k - 1], pg_send.at[k - 1], pg_recv.at[k - 1], plane(-k), z)
        for k in range(1, stops + 1)
    ]
    for copy in pg_copies:
        copy.start()

    def negatives(t, carry):
        i = t // n_rep
        at = pl.ds(pl.multiple_of(t * edges, edges), edges)
        scores = lax.dot_general(wide[at, :], neg[i], by_row, preferred_element_type=F32)
        neg_grad = (weight * jax.nn.sigmoid(scores)).astype(BF16)
        pull = jnp.dot(neg_grad, neg[i], preferred_element_type=F32)
        pulled[at, :] = (pull * rel[pl.ds(first_stop + i, 1), :]).astype(BF16)
        return carry

    cuts = rs_recv.shape[1]
    cut_rows = rows // cuts

    def rs_copy(to, cut):
        at = pl.ds(cut * cut_rows, cut_rows)
        return remote(
            give.at[to, at], take.at[z - 1, at], rs_send.at[to, cut], rs_recv.at[z - 1, cut], b, to
        )

    @pl.when(inner)
    def _():
        sib_copy.wait()
        lax.fori_loop(0, 2 * n_rep, negatives, 0)
        for cut in range(cuts):
            at = pl.ds(cut * cut_rows, cut_rows)
            summed = jnp.dot(spread[at, :], pulled[...], preferred_element_type=F32)
            for to in (0, 3, 1, 2):
                chunk = summed[:, to * width : (to + 1) * width]
                give[to, at, :] = chunk.astype(BF16)

                @pl.when(z != to)
                def _():
                    rs_copy(to, cut).start()

                @pl.when(z == to)
                def _():
                    out_ref[at, :] = chunk

    @pl.when(jnp.logical_not(inner))
    def _():
        out_ref[...] = jnp.zeros_like(out_ref)

    lax.fori_loop(0, stops, gather_incoming, 0)

    def scatter_home(s, carry):
        total = jnp.zeros((rows, width), F32)
        for r in range(n_rep):
            t = s * n_rep + r
            hot = by_entity(idz[r, pl.ds(s, 1), :], rows, pos_grad[pl.ds(t, 1), :])
            rows_in = (ctx[t].astype(F32) * rel_wide[s]).astype(BF16)
            total = total + lax.dot_general(hot, rows_in, by_row, preferred_element_type=F32)
        out_ref[...] += total
        return carry

    lax.fori_loop(0, stops, scatter_home, 0)
    for copy in pg_copies:
        copy.wait()

    def scatter_incoming(s, carry):
        total = jnp.zeros((rows, width), F32)
        for r in range(n_rep):
            t = s * n_rep + r
            hot = by_entity(idn[s, r, pl.ds(stops + s, 1), :], rows, pos_in[s, pl.ds(t, 1), :])
            total = total + lax.dot_general(hot, his[t], by_row, preferred_element_type=F32)
        out_ref[...] += total
        return carry

    lax.fori_loop(0, stops, scatter_incoming, 0)
    for source in (1, 2):

        @pl.when(z != source)
        def _():
            for cut in range(cuts):
                at = pl.ds(cut * cut_rows, cut_rows)
                remote(
                    give.at[0, at], take.at[source - 1, at], rs_send.at[0, cut], rs_recv.at[source - 1, cut],
                    b, source,
                ).wait_recv()
            out_ref[...] += take[source - 1].astype(F32)

    @pl.when(inner)
    def _():
        for to in range(n_rep):

            @pl.when(z != to)
            def _():
                for cut in range(cuts):
                    rs_copy(to, cut).wait_send()


def fused(n_blk, n_rep, embeddings, relation, head_ids, context_ids, neg_owner, neg_ids):
    rows, dim = embeddings.shape
    stops, edges = head_ids.shape
    negs = neg_ids.shape[1]
    width = dim // n_rep
    blocks = stops * n_rep
    hbm = pl.BlockSpec(memory_space=pl.ANY)
    dma = pltpu.SemaphoreType.DMA
    return pl.pallas_call(
        functools.partial(kernel, n_blk, n_rep, 4.0 / negs),
        out_shape=jax.ShapeDtypeStruct((rows, width), F32),
        in_specs=[pl.BlockSpec(memory_space=pltpu.SMEM)] + [hbm] * 5,
        out_specs=pl.BlockSpec(memory_space=pltpu.VMEM),
        scratch_shapes=[
            pltpu.VMEM((rows, dim), BF16),
            pltpu.VMEM((stops, dim), F32),
            pltpu.VMEM((stops, negs), jnp.int32),
            dma((5,)),
            pltpu.VMEM((n_blk, width, rows), BF16),
            pltpu.VMEM((n_rep, 2 * stops, edges), jnp.int32),
            pltpu.VMEM((stops, n_rep, 2 * stops, edges), jnp.int32),
            pltpu.VMEM((blocks, width, edges), BF16),
            pltpu.VMEM((blocks, width, edges), BF16),
            pltpu.VMEM((blocks, width, edges), BF16),
            pltpu.VMEM((n_rep, blocks, edges), F32),
            pltpu.VMEM((blocks, edges), F32),
            pltpu.VMEM((stops, blocks, edges), F32),
            pltpu.VMEM((stops, negs // 2, rows), BF16),
            pltpu.VMEM((stops, negs // 2, width), BF16),
            pltpu.VMEM((2, negs, dim), BF16),
            pltpu.VMEM((2 * n_rep * edges, dim), BF16),
            pltpu.VMEM((rows, 2 * n_rep * edges), BF16),
            pltpu.VMEM((n_rep, rows, width), BF16),
            pltpu.VMEM((2, rows, width), BF16),
            pltpu.VMEM((2 * n_rep * edges, dim), BF16),
            pltpu.VMEM((stops, width, edges), F32),
            dma((n_blk // 2,)), dma((n_blk // 2,)), dma((n_blk // 2,)), dma((n_blk // 2,)),
            dma((n_rep,)), dma((n_rep,)), dma((stops,)), dma((stops,)),
            dma((n_rep,)), dma((n_rep,)), dma((stops,)), dma((stops,)),
            dma((stops,)), dma((2, n_rep)), dma, dma, dma((n_rep, 4)), dma((2, 4)),
        ],
        compiler_params=pltpu.CompilerParams(
            collective_id=0, has_side_effects=True, vmem_limit_bytes=52 * 1024 * 1024
        ),
    )(neg_owner, embeddings, relation, head_ids, context_ids, neg_ids)


def shifted(shard, axis, by):
    peers = lax.axis_size(axis)
    return lax.ppermute(shard, axis, [(i, (i + by) % peers) for i in range(peers)])


def broadcast(value, axis, source):
    kept = jnp.where(lax.axis_index(axis) == source, value, 0).astype(value.dtype)
    return lax.psum(kept, axis)


def stop_terms(home_rows, visitor, negatives, relation_row, head_index, context_index, weight):
    head_rows = jnp.take(home_rows, head_index, axis=0)
    context_rows = jnp.take(visitor, context_index, axis=0)
    weighted = (head_rows.astype(jnp.float32) * relation_row).astype(jnp.bfloat16)
    positive = jnp.sum(weighted.astype(jnp.float32) * context_rows.astype(jnp.float32), axis=1)
    scores = lax.dot_general(
        weighted, negatives, (((1,), (1,)), ((), ())), preferred_element_type=jnp.float32
    )
    pos_grad = -jax.nn.sigmoid(-positive)
    neg_grad = (weight * jax.nn.sigmoid(scores)).astype(jnp.bfloat16)
    pulled = jnp.dot(neg_grad, negatives, preferred_element_type=jnp.float32)
    head_terms = relation_row * (pos_grad[:, None] * context_rows.astype(jnp.float32) + pulled)
    context_terms = pos_grad[:, None] * weighted.astype(jnp.float32)
    empty = jnp.zeros((home_rows.shape[0], home_rows.shape[1]), jnp.float32)
    return (empty.at[head_index].add(head_terms), empty.at[context_index].add(context_terms))


def by_collectives(embeddings, relation, head_ids, context_ids, neg_owner, neg_ids):
    weight = 4.0 / neg_ids.shape[1]
    stop_count = head_ids.shape[0]
    visitor = embeddings
    head_total = jnp.zeros(embeddings.shape, jnp.float32)
    returned = jnp.zeros(embeddings.shape, jnp.float32)
    for stop_index in range(stop_count):
        visitor = shifted(visitor, "blk", 1)
        owner = neg_owner[stop_index]
        picked = jnp.take(embeddings, neg_ids[stop_index], axis=0)
        negatives = broadcast(picked, "blk", owner)
        head_part, context_part = stop_terms(
            embeddings,
            visitor,
            negatives,
            relation[stop_index],
            head_ids[stop_index],
            context_ids[stop_index],
            weight,
        )
        head_total = head_total + head_part
        returned = returned + shifted(
            context_part.astype(jnp.bfloat16), "blk", -(stop_index + 1)
        ).astype(context_part.dtype)
    combined = head_total + returned
    return lax.psum_scatter(combined, "rep", scatter_dimension=1, tiled=True)


def per_device(n_blk, n_rep, embeddings, relation, head_ids, context_ids, neg_owner, neg_ids):
    rows, dim = embeddings.shape
    stops = head_ids.shape[0]
    fits = n_blk * rows * (dim // n_rep) * 2 <= 8 * 1024 * 1024
    if fits and n_rep == stops == 4 and n_blk > stops and n_blk % 2 == 0:
        return fused(n_blk, n_rep, embeddings, relation, head_ids, context_ids, neg_owner, neg_ids)
    return by_collectives(embeddings, relation, head_ids, context_ids, neg_owner, neg_ids)


def solution(mesh):
    in_specs = (P("blk", None), P(), P(None, ("blk", "rep")), P(None, ("blk", "rep")), P(), P())
    out_specs = P("blk", "rep")
    return jax.shard_map(
        functools.partial(per_device, mesh.shape["blk"], mesh.shape["rep"]), mesh=mesh, in_specs=in_specs, out_specs=out_specs, check_vma=False
    )
```
